512 devices in a mesh: prow: 16 (over x, z_hi), pcol: 32 (over z_lo, y, core).
Axes of the slice: x: 4, y: 4, z: 16 (z_hi: 4, z_lo: 4; z = z_hi * 4 + z_lo), core: 2. Of those that a mesh axis runs over, the one named last changes fastest.
Arguments:
- panel: float32 [4096, 4096], P('pcol', 'prow'), may hold values from -1.2 to 1.2
- ancestor_inverse: float32 [4096, 4096], P('prow', 'pcol'), as said below
- diag_inverse: float32 [4096, 2048], P(('prow', 'pcol')), may hold values from -6 to 6
- pattern: int32 [32, 32], replicated, may hold values from 0 to 1, as said below
Outputs:
- inverse_rows: float32 [4096, 4096], P('prow', 'pcol')
- diag_blocks: float32 [4096, 2048], P(('prow', 'pcol'))
The draws below stay inside these ranges and needn't reach their ends.
Inputs may be any that keep to these rules, and one draw needn't show every extreme that they name: pattern[i, j] is 1 where block (i, j) of 128 x 128 entries of the panel is structurally nonzero, else 0. ancestor_inverse is symmetric.
All inputs are finite; a program needn't handle non-finite values.
Results may differ from the reference program's by a relative error of at most 0.0001.
Values sent between devices are 32-bit elements; how exact they have to be, the bound alone decides.
No kernel may reach another device: no remote copies, remote signals or barrier semaphores. Data moves between devices by JAX's collectives and lax.ppermute only.
A program may use at most 64 MiB of HBM per device.

```python
import jax
import jax.numpy as jnp
from jax import lax

BLOCK = 128
WB = 2048
SIBS = 2
CHAIN = 4096


def draw_ancestor_inverse(key, part):
    key = jax.random.fold_in(key, 11)
    entries = jax.random.normal(key, (CHAIN, CHAIN), jnp.float32)
    symmetric = (entries + entries.T) * (0.70710678 * CHAIN ** (-0.5))
    return symmetric + jnp.eye(CHAIN, dtype=jnp.float32)


def draw_pattern(key, part):
    key = jax.random.fold_in(key, 23)
    block_rows = SIBS * WB // BLOCK
    block_cols = CHAIN // BLOCK
    ancestor_level = lax.iota(jnp.int32, block_cols) // (WB // BLOCK)
    threshold = 3 + 2 * ancestor_level
    integers = jax.random.randint(key, (block_rows, block_cols), 0, 10)
    return (integers < threshold[None, :]).astype(jnp.int32)


def levels(own_key, dims, split, smallest, high):
    loudness = 1.0
    for axis_at, shards_of in split:
        heights = jax.random.uniform(jax.random.fold_in(jax.random.fold_in(own_key, 6), axis_at), (shards_of,), jnp.float32, smallest / len(split), high / len(split))
        loudness = loudness * jnp.repeat(jnp.exp(heights), dims[axis_at] // shards_of).reshape((-1,) + (1,) * (len(dims) - 1 - axis_at))
    return loudness


def centred(rng, dims, spread, most, shards=(), kind=jnp.bfloat16):
    values = spread * jax.random.normal(rng, dims, jnp.float32)
    if shards:
        values = values * levels(rng, dims, shards, -0.22, 0.18)
    return jnp.clip(values, -most, most).astype(kind)


def setup_inputs(seed: int = 0) -> dict:
    arg_keys = jax.random.split(jax.random.key(seed), 5)
    panel = centred(arg_keys[0], (SIBS * WB, CHAIN), 0.2, 1.2, ((0, 32), (1, 16)), jnp.float32)
    ancestor_inverse = draw_ancestor_inverse(jax.random.fold_in(arg_keys[4], 71), 0)
    diag_inverse = centred(arg_keys[2], (SIBS * WB, WB), 1.0, 6.0, ((0, 512),), jnp.float32)
    pattern = draw_pattern(jax.random.fold_in(arg_keys[4], 71), 0)
    return dict(panel=panel, ancestor_inverse=ancestor_inverse, diag_inverse=diag_inverse, pattern=pattern)


def expand_pattern(pattern):
    pattern_float = pattern.astype(jnp.float32)
    return jnp.repeat(jnp.repeat(pattern_float, BLOCK, axis=0), BLOCK, axis=1)


def reference(panel, ancestor_inverse, diag_inverse, pattern):
    masked = panel * expand_pattern(pattern)
    inverse_rows = -jnp.dot(masked, ancestor_inverse, precision=lax.Precision.HIGHEST, preferred_element_type=jnp.float32)
    pieces = []
    for sibling in range(SIBS):
        row_start = sibling * WB
        sibling_rows = inverse_rows[row_start:row_start + WB]
        sibling_panel = masked[row_start:row_start + WB]
        pieces.append(lax.dot_general(sibling_rows, sibling_panel, (((1,), (1,)), ((), ())), precision=lax.Precision.HIGHEST, preferred_element_type=jnp.float32))
    coupling = jnp.concatenate(pieces, axis=0)
    return inverse_rows, diag_inverse - coupling
```

```python
import jax
import jax.numpy as jnp
from jax import lax
from jax.sharding import Mesh, PartitionSpec as P

AXES = ("x", "zh", "zl", "y", "c")
SIZES = (4, 4, 4, 4, 2)
high = lax.Precision.HIGH


def flat(x, zh, zl, y, c):
    return (((x * 4 + zh) * 4 + zl) * 4 + y) * 2 + c


def everyone():
    return [
        (x, zh, zl, y, c)
        for x in range(4)
        for zh in range(4)
        for zl in range(4)
        for y in range(4)
        for c in range(2)
    ]


def shift_pairs(step):
    return [(i, (i + step) % 4) for i in range(4)]


def column_form_pairs(step):
    return [
        (flat(x, zh, zl, y, c), flat(zl, (y + step) % 4, x, zh, c))
        for x, zh, zl, y, c in everyone()
    ]


def pick(blocks, index):
    return lax.dynamic_index_in_dim(blocks, index, 0, keepdims=False)


def on_device(panel, ancestor_inverse, diag_inverse, pattern):
    x = lax.axis_index("x")
    zh = lax.axis_index("zh")
    zl = lax.axis_index("zl")
    y = lax.axis_index("y")
    c = lax.axis_index("c")

    own = lax.dynamic_slice(
        pattern, ((zl * 4 + y) * 2 + c, (x * 4 + zh) * 2), (1, 2)
    ).astype(jnp.float32)
    masked = panel * jnp.repeat(own, 128, axis=1)

    a_cols = lax.all_gather(ancestor_inverse, "c", axis=1, tiled=True)

    over_zl = lax.all_gather(masked, "zl", axis=0, tiled=True)

    col_blocks = [
        lax.ppermute(masked, AXES, column_form_pairs(t)) for t in range(4)
    ]

    by_y = [over_zl] + [
        lax.ppermute(over_zl, "y", shift_pairs(s)) for s in (1, 2, 3)
    ]
    gathered = jnp.stack([g.reshape(4, 128, 256) for g in by_y], axis=1)
    partial = jnp.dot(
        gathered.reshape(2048, 256), a_cols, precision=high,
        preferred_element_type=jnp.float32,
    )
    over_x = lax.all_to_all(partial, "x", 0, 0, tiled=True)
    sum_x = jnp.sum(over_x.reshape(4, 4, 128, 256), axis=0)
    ordered = jnp.stack([pick(sum_x, (y - b) % 4) for b in range(4)])
    over_zh = lax.all_to_all(ordered, "zh", 0, 0, tiled=True)
    half_rows = -jnp.sum(over_zh, axis=0)
    rows = lax.all_gather(half_rows, "c", axis=0, tiled=True)
    inverse_rows = lax.dynamic_slice_in_dim(rows, c * 128, 128, 1)

    col_half = jnp.concatenate(col_blocks, axis=0)
    col_other = lax.ppermute(col_half, "x", [(i, i ^ 1) for i in range(4)])
    col_form = jnp.concatenate([col_half, col_other], axis=0)

    lhs = rows.reshape(4, 4, 16, 256).transpose(1, 0, 2, 3).reshape(256, 256)
    coupling = lax.dot_general(
        lhs, col_form, (((1,), (1,)), ((), ())), precision=high,
        preferred_element_type=jnp.float32,
    )
    over_y = lax.all_to_all(coupling, "y", 0, 0, tiled=True)
    sum_y = jnp.sum(over_y.reshape(4, 64, 1024), axis=0)
    over_l = lax.all_to_all(sum_y, "zl", 0, 0, tiled=True)
    sum_l = jnp.sum(over_l.reshape(4, 16, 1024), axis=0)
    both = lax.all_to_all(sum_l, "c", 0, 0, tiled=True).reshape(2, 8, 2, 4, 128)
    blocks = both.transpose(2, 3, 1, 0, 4)
    blocks = jnp.stack([pick(blocks, (b + x) % 2) for b in range(2)])
    blocks = jnp.stack(
        [
            lax.dynamic_index_in_dim(blocks, (zh - b) % 4, 1, keepdims=False)
            for b in range(4)
        ],
        axis=1,
    )
    total = blocks.transpose(2, 0, 1, 3, 4).reshape(8, 2048)
    return (inverse_rows, diag_inverse - total)


def solution(mesh):
    fine = Mesh(mesh.devices.reshape(SIZES), AXES)
    prow, pcol = ("x", "zh"), ("zl", "y", "c")
    return jax.shard_map(
        on_device,
        mesh=fine,
        in_specs=(P(pcol, prow), P(prow, pcol), P(AXES, None), P()),
        out_specs=(P(prow, pcol), P(AXES, None)),
        check_vma=False,
    )
```

```python
import jax
import jax.numpy as jnp
from jax import lax
from jax.sharding import Mesh, PartitionSpec as P

AXES = ("x", "zh", "zl", "y", "c")
SIZES = (4, 4, 4, 4, 2)
high = lax.Precision.HIGH


def turn_pairs():
    def flat(x, zh, zl, rest):
        return ((x * 4 + zh) * 4 + zl) * 8 + rest

    return [
        (flat(x, zh, zl, rest), flat(zl, zh, x, rest))
        for x in range(4)
        for zh in range(4)
        for zl in range(4)
        for rest in range(8)
    ]


def shift_pairs(step):
    return [(i, (i + step) % 4) for i in range(4)]


def pick(blocks, index, axis=0):
    return lax.dynamic_index_in_dim(blocks, index, axis, keepdims=False)


def dot(lhs, rhs, dims):
    return lax.dot_general(
        lhs, rhs, (dims, ((), ())), precision=high,
        preferred_element_type=jnp.float32,
    )


def on_device(panel, ancestor_inverse, diag_inverse, pattern):
    x = lax.axis_index("x")
    zh = lax.axis_index("zh")
    zl = lax.axis_index("zl")
    y = lax.axis_index("y")
    c = lax.axis_index("c")

    moved = lax.ppermute(panel, AXES, turn_pairs())
    own = lax.dynamic_slice(
        pattern, ((x * 4 + y) * 2 + c, (zl * 4 + zh) * 2), (1, 2)
    ).astype(jnp.float32)
    moved = moved * jnp.repeat(own, 128, axis=1)

    a_own = lax.all_gather(ancestor_inverse, "x", axis=0, tiled=True)
    a_other = lax.ppermute(a_own, "c", [(0, 1), (1, 0)])

    moved, a_own = lax.optimization_barrier((moved, a_own))
    over_zl = lax.all_gather(moved, "zl", axis=0)
    over_zl = over_zl.transpose(1, 0, 2).reshape(128, 1024)
    copies = lax.optimization_barrier(jnp.stack([over_zl] * 4))
    by_y = lax.all_to_all(copies, "y", 0, 0, tiled=True).reshape(512, 1024)

    moved, _ = lax.optimization_barrier((moved, copies))
    over_zh = lax.all_gather(moved, "zh", axis=0)
    by_y, over_zh = lax.optimization_barrier((by_y, over_zh))

    partial = jnp.concatenate(
        [dot(by_y, a, ((1,), (0,))) for a in (a_own, a_other)], axis=1
    )
    summed = lax.all_to_all(partial, "zh", 0, 0, tiled=True)
    summed = -jnp.sum(summed.reshape(4, 128, 256), axis=0)

    over_zh, _ = lax.optimization_barrier((over_zh, partial))
    pieces = [pick(over_zh, y)] + [
        lax.ppermute(pick(over_zh, (y + s) % 4), "y", shift_pairs(s))
        for s in (1, 2, 3)
    ]
    pieces = jnp.stack(pieces)
    col_half = jnp.concatenate([pick(pieces, (y - b) % 4) for b in range(4)])
    col_other = lax.ppermute(col_half, "x", [(i, i ^ 1) for i in range(4)])
    col_form = jnp.concatenate([col_half, col_other], axis=0)

    crossed = jnp.concatenate([summed[:, 128:], summed[:, :128]], axis=1)
    half_rows = jnp.where(c == 0, summed, crossed)
    rows = lax.all_gather(half_rows, "c", axis=0, tiled=True)
    inverse_rows = lax.dynamic_slice_in_dim(rows, c * 128, 128, 1)

    lhs = rows.reshape(4, 4, 16, 256).transpose(1, 0, 2, 3).reshape(256, 256)
    coupling = dot(lhs, col_form, ((1,), (1,)))
    over_y = lax.all_to_all(coupling, "y", 0, 0, tiled=True)
    sum_y = jnp.sum(over_y.reshape(4, 64, 1024), axis=0)
    over_l = lax.all_to_all(sum_y, ("zl", "c"), 0, 0, tiled=True)
    both = jnp.sum(over_l.reshape(4, 2, 8, 2, 4, 128), axis=0)
    both = both.transpose(2, 1, 3, 0, 4)
    both = jnp.stack([pick(both, (b + x) % 2) for b in range(2)], axis=1)
    return (inverse_rows, diag_inverse - both.reshape(8, 2048))


def solution(mesh):
    fine = Mesh(mesh.devices.reshape(SIZES), AXES)
    prow, pcol = ("x", "zh"), ("zl", "y", "c")
    return jax.shard_map(
        on_device,
        mesh=fine,
        in_specs=(P(pcol, prow), P(prow, pcol), P(AXES, None), P()),
        out_specs=(P(prow, pcol), P(AXES, None)),
        check_vma=False,
    )
```

```python
import jax
import jax.numpy as jnp
from jax import lax
from jax.sharding import Mesh, PartitionSpec as P

AXES = ("x", "zh", "zl", "y", "c")
SIZES = (4, 4, 4, 4, 2)
high = lax.Precision.HIGH


def turn_pairs():
    def flat(x, zh, zl, rest):
        return ((x * 4 + zh) * 4 + zl) * 8 + rest

    return [
        (flat(x, zh, zl, rest), flat(zl, zh, x, rest))
        for x in range(4)
        for zh in range(4)
        for zl in range(4)
        for rest in range(8)
    ]


def shift_pairs(step):
    return [(i, (i + step) % 4) for i in range(4)]


def pick(blocks, index, axis=0):
    return lax.dynamic_index_in_dim(blocks, index, axis, keepdims=False)


def dot(lhs, rhs, dims):
    return lax.dot_general(
        lhs, rhs, (dims, ((), ())), precision=high,
        preferred_element_type=jnp.float32,
    )


def on_device(panel, ancestor_inverse, diag_inverse, pattern):
    x = lax.axis_index("x")
    zh = lax.axis_index("zh")
    zl = lax.axis_index("zl")
    y = lax.axis_index("y")
    c = lax.axis_index("c")

    moved = lax.ppermute(panel, AXES, turn_pairs())
    own = lax.dynamic_slice(
        pattern, ((x * 4 + y) * 2 + c, (zl * 4 + zh) * 2), (1, 2)
    ).astype(jnp.float32)
    moved = moved * jnp.repeat(own, 128, axis=1)

    a_cols = lax.all_gather(ancestor_inverse, "c", axis=0)
    a_cols = jnp.concatenate([a_cols[0], a_cols[1]], axis=1)
    a_copies = lax.optimization_barrier(jnp.stack([a_cols] * 4))
    a_all = lax.all_to_all(a_copies, "x", 0, 0, tiled=True).reshape(1024, 256)

    moved, _ = lax.optimization_barrier((moved, a_copies))
    over_zl = lax.all_gather(moved, "zl", axis=0)
    over_zl, a_all = lax.optimization_barrier((over_zl, a_all))
    over_zl = over_zl.transpose(1, 0, 2).reshape(128, 1024)
    copies = lax.optimization_barrier(jnp.stack([over_zl] * 4))
    by_y = lax.all_to_all(copies, "y", 0, 0, tiled=True).reshape(512, 1024)

    moved, _ = lax.optimization_barrier((moved, copies))
    over_zh = lax.all_gather(moved, "zh", axis=0)
    by_y, over_zh = lax.optimization_barrier((by_y, over_zh))
    pair_zh = lax.ppermute(over_zh, "x", [(i, i ^ 1) for i in range(4)])

    partial = dot(by_y, a_all, ((1,), (0,)))
    summed = lax.all_to_all(partial, "zh", 0, 0, tiled=True)
    summed = -jnp.sum(summed.reshape(4, 128, 256), axis=0)

    def column(index):
        return jnp.concatenate([pick(over_zh, index), pick(pair_zh, index)])

    over_zh, pair_zh, _ = lax.optimization_barrier((over_zh, pair_zh, partial))
    pieces = [column(y)] + [
        lax.ppermute(column((y + s) % 4), "y", shift_pairs(s)) for s in (1, 2, 3)
    ]
    pieces = jnp.stack(pieces).reshape(4, 2, 128, 256)
    col_form = jnp.stack([pick(pieces, (y - b) % 4) for b in range(4)], axis=1)
    col_form = col_form.reshape(1024, 256)

    rows = lax.all_gather(summed, "c", axis=0, tiled=True)
    inverse_rows = lax.dynamic_slice_in_dim(rows, c * 128, 128, 1)

    lhs = rows.reshape(4, 4, 16, 256).transpose(1, 0, 2, 3).reshape(256, 256)
    coupling = dot(lhs, col_form, ((1,), (1,)))
    over_y = lax.all_to_all(coupling, "y", 0, 0, tiled=True)
    sum_y = jnp.sum(over_y.reshape(4, 64, 1024), axis=0)
    over_l = lax.all_to_all(sum_y, ("zl", "c"), 0, 0, tiled=True)
    both = jnp.sum(over_l.reshape(4, 2, 8, 2, 4, 128), axis=0)
    both = both.transpose(2, 1, 3, 0, 4)
    both = jnp.stack([pick(both, (b + x) % 2) for b in range(2)], axis=1)
    return (inverse_rows, diag_inverse - both.reshape(8, 2048))


def solution(mesh):
    fine = Mesh(mesh.devices.reshape(SIZES), AXES)
    prow, pcol = ("x", "zh"), ("zl", "y", "c")
    return jax.shard_map(
        on_device,
        mesh=fine,
        in_specs=(P(pcol, prow), P(prow, pcol), P(AXES, None), P()),
        out_specs=(P(prow, pcol), P(AXES, None)),
        check_vma=False,
    )
```

```python
import jax
import jax.numpy as jnp
from jax import lax
from jax.sharding import Mesh, PartitionSpec as P

AXES = ("x", "zh", "zl", "y", "c")
SIZES = (4, 4, 4, 4, 2)
high = lax.Precision.HIGH


def turn_pairs():
    def flat(x, zh, zl, rest):
        return ((x * 4 + zh) * 4 + zl) * 8 + rest

    return [
        (flat(x, zh, zl, rest), flat(zl, zh, x, rest))
        for x in range(4)
        for zh in range(4)
        for zl in range(4)
        for rest in range(8)
    ]


def shift_pairs(step):
    return [(i, (i + step) % 4) for i in range(4)]


def pick(blocks, index, axis=0):
    return lax.dynamic_index_in_dim(blocks, index, axis, keepdims=False)


def dot(lhs, rhs, dims):
    return lax.dot_general(
        lhs, rhs, (dims, ((), ())), precision=high,
        preferred_element_type=jnp.float32,
    )


def on_device(panel, ancestor_inverse, diag_inverse, pattern):
    x = lax.axis_index("x")
    zh = lax.axis_index("zh")
    zl = lax.axis_index("zl")
    y = lax.axis_index("y")
    c = lax.axis_index("c")

    moved = lax.ppermute(panel, AXES, turn_pairs())
    own = lax.dynamic_slice(
        pattern, ((x * 4 + y) * 2 + c, (zl * 4 + zh) * 2), (1, 2)
    ).astype(jnp.float32)
    moved = moved * jnp.repeat(own, 128, axis=1)

    a_cols = lax.all_gather(ancestor_inverse, "c", axis=0)
    a_cols = jnp.concatenate([a_cols[0], a_cols[1]], axis=1)
    a_copies, moved = lax.optimization_barrier((jnp.stack([a_cols] * 4), moved))
    a_all = lax.all_to_all(a_copies, "x", 0, 0, tiled=True).reshape(1024, 256)

    over_zl = lax.all_gather(moved, "zl", axis=0)
    over_zl, a_all = lax.optimization_barrier((over_zl, a_all))
    over_zl = over_zl.transpose(1, 0, 2).reshape(128, 1024)
    copies = lax.optimization_barrier(jnp.stack([over_zl] * 4))
    by_y = lax.all_to_all(copies, "y", 0, 0, tiled=True).reshape(512, 1024)

    moved, _ = lax.optimization_barrier((moved, copies))
    over_zh = lax.all_gather(moved, "zh", axis=0)
    by_y, over_zh = lax.optimization_barrier((by_y, over_zh))
    pair_zh = lax.ppermute(over_zh, "x", [(i, i ^ 1) for i in range(4)])

    partial = dot(by_y, a_all, ((1,), (0,)))
    summed = lax.all_to_all(partial, "zh", 0, 0, tiled=True)
    summed = -jnp.sum(summed.reshape(4, 128, 256), axis=0)

    def column(index):
        return jnp.concatenate([pick(over_zh, index), pick(pair_zh, index)])

    over_zh, pair_zh, _ = lax.optimization_barrier((over_zh, pair_zh, partial))
    pieces = [column(y)] + [
        lax.ppermute(column((y + s) % 4), "y", shift_pairs(s)) for s in (1, 2, 3)
    ]
    pieces = jnp.stack(pieces).reshape(4, 2, 128, 256)
    col_form = jnp.stack([pick(pieces, (y - b) % 4) for b in range(4)], axis=1)
    col_form = col_form.reshape(1024, 256)

    rows = lax.all_gather(summed, "c", axis=0, tiled=True)
    inverse_rows = lax.dynamic_slice_in_dim(rows, c * 128, 128, 1)

    lhs = rows.reshape(4, 4, 16, 256).transpose(1, 0, 2, 3).reshape(256, 256)
    coupling = dot(lhs, col_form, ((1,), (1,)))
    over_y = lax.all_to_all(coupling, "y", 0, 0, tiled=True)
    sum_y = jnp.sum(over_y.reshape(4, 64, 1024), axis=0)
    over_l = lax.all_to_all(sum_y, ("zl", "c"), 0, 0, tiled=True)
    both = jnp.sum(over_l.reshape(4, 2, 8, 2, 4, 128), axis=0)
    both = both.transpose(2, 1, 3, 0, 4)
    both = jnp.stack([pick(both, (b + x) % 2) for b in range(2)], axis=1)
    return (inverse_rows, diag_inverse - both.reshape(8, 2048))


def solution(mesh):
    fine = Mesh(mesh.devices.reshape(SIZES), AXES)
    prow, pcol = ("x", "zh"), ("zl", "y", "c")
    return jax.shard_map(
        on_device,
        mesh=fine,
        in_specs=(P(pcol, prow), P(prow, pcol), P(AXES, None), P()),
        out_specs=(P(prow, pcol), P(AXES, None)),
        check_vma=False,
    )
```

```python
import jax
import jax.numpy as jnp
from jax import lax
from jax.sharding import Mesh, PartitionSpec as P

AXES = ("x", "zh", "zl", "y", "c")
SIZES = (4, 4, 4, 4, 2)
high = lax.Precision.HIGH


def turn_pairs():
    def flat(x, zh, zl, rest):
        return ((x * 4 + zh) * 4 + zl) * 8 + rest

    return [
        (flat(x, zh, zl, rest), flat(zl, zh, x, rest))
        for x in range(4)
        for zh in range(4)
        for zl in range(4)
        for rest in range(8)
    ]


def shift_pairs(step):
    return [(i, (i + step) % 4) for i in range(4)]


def pick(blocks, index, axis=0):
    return lax.dynamic_index_in_dim(blocks, index, axis, keepdims=False)


def dot(lhs, rhs, dims):
    return lax.dot_general(
        lhs, rhs, (dims, ((), ())), precision=high,
        preferred_element_type=jnp.float32,
    )


def on_device(panel, ancestor_inverse, diag_inverse, pattern):
    x = lax.axis_index("x")
    zh = lax.axis_index("zh")
    zl = lax.axis_index("zl")
    y = lax.axis_index("y")
    c = lax.axis_index("c")

    moved = lax.ppermute(panel, AXES, turn_pairs())

    def pattern_row(x):
        row = lax.dynamic_slice_in_dim(pattern, (x * 4 + y) * 2 + c, 1, 0)
        return row.astype(jnp.float32).reshape(4, 4, 2)

    row, pair_row = pattern_row(x), pattern_row(x ^ 1)
    mask = jnp.repeat(pick(row, zh, 1), 128, axis=1)[:, None, :]
    masks = [jnp.repeat(pick(r, zl), 128, axis=1)[:, None, :] for r in (row, pair_row)]

    a_cols = lax.all_gather(ancestor_inverse, "c", axis=0)
    a_cols = jnp.concatenate([a_cols[0], a_cols[1]], axis=1)
    a_copies, moved, mask, masks = lax.optimization_barrier(
        (jnp.stack([a_cols] * 4), moved, mask, masks)
    )
    a_all = lax.all_to_all(a_copies, "x", 0, 0, tiled=True).reshape(1024, 256)

    over_zl = lax.all_gather(moved, "zl", axis=0)
    over_zl, a_all = lax.optimization_barrier((over_zl, a_all))
    over_zl = over_zl * mask
    copies = lax.optimization_barrier(jnp.stack([over_zl] * 4))
    by_y = lax.all_to_all(copies, "y", 0, 0, tiled=True)

    moved, _ = lax.optimization_barrier((moved, copies))
    over_zh = lax.all_gather(moved, "zh", axis=0)
    by_y, over_zh = lax.optimization_barrier((by_y, over_zh))
    pair_zh = lax.ppermute(over_zh, "x", [(i, i ^ 1) for i in range(4)])

    partial = sum(
        dot(
            by_y[:, k].reshape(512, 256), a_all[256 * k : 256 * (k + 1)],
            ((1,), (0,)),
        )
        for k in range(4)
    )
    summed = lax.all_to_all(partial, "zh", 0, 0, tiled=True)
    summed = -jnp.sum(summed.reshape(4, 128, 256), axis=0)

    def column(index):
        pair = (over_zh, pair_zh)
        return jnp.concatenate(
            [pick(b, index) * pick(m, index) for b, m in zip(pair, masks)]
        )

    over_zh, pair_zh, _ = lax.optimization_barrier((over_zh, pair_zh, partial))
    pieces = [column(y)] + [
        lax.ppermute(column((y + s) % 4), "y", shift_pairs(s)) for s in (1, 2, 3)
    ]
    pieces = jnp.stack(pieces).reshape(4, 2, 128, 256)
    col_form = jnp.stack([pick(pieces, (y - b) % 4) for b in range(4)], axis=1)
    col_form = col_form.reshape(1024, 256)

    rows = lax.all_gather(summed, "c", axis=0, tiled=True)
    inverse_rows = lax.dynamic_slice_in_dim(rows, c * 128, 128, 1)

    lhs = rows.reshape(4, 4, 16, 256).transpose(1, 0, 2, 3).reshape(256, 256)
    coupling = dot(lhs, col_form, ((1,), (1,)))
    over_y = lax.all_to_all(coupling, "y", 0, 0, tiled=True)
    sum_y = jnp.sum(over_y.reshape(4, 64, 1024), axis=0)
    over_l = lax.all_to_all(sum_y, ("zl", "c"), 0, 0, tiled=True)
    both = jnp.sum(over_l.reshape(4, 2, 8, 2, 4, 128), axis=0)
    both = both.transpose(2, 1, 3, 0, 4)
    both = jnp.stack([pick(both, (b + x) % 2) for b in range(2)], axis=1)
    return (inverse_rows, diag_inverse - both.reshape(8, 2048))


def solution(mesh):
    fine = Mesh(mesh.devices.reshape(SIZES), AXES)
    prow, pcol = ("x", "zh"), ("zl", "y", "c")
    return jax.shard_map(
        on_device,
        mesh=fine,
        in_specs=(P(pcol, prow), P(prow, pcol), P(AXES, None), P()),
        out_specs=(P(prow, pcol), P(AXES, None)),
        check_vma=False,
    )
```

```python
import jax
import jax.numpy as jnp
from jax import lax
from jax.sharding import Mesh, PartitionSpec as P

AXES = ("x", "zh", "zl", "y", "c")
SIZES = (4, 4, 4, 4, 2)
high = lax.Precision.HIGH


def turn_pairs():
    def flat(x, zh, zl, rest):
        return ((x * 4 + zh) * 4 + zl) * 8 + rest

    return [
        (flat(x, zh, zl, rest), flat(zl, zh, x, rest))
        for x in range(4)
        for zh in range(4)
        for zl in range(4)
        for rest in range(8)
    ]


def shift_pairs(step):
    return [(i, (i + step) % 4) for i in range(4)]


def pick(blocks, index, axis=0):
    return lax.dynamic_index_in_dim(blocks, index, axis, keepdims=False)


def dot(lhs, rhs, dims):
    return lax.dot_general(
        lhs, rhs, (dims, ((), ())), precision=high,
        preferred_element_type=jnp.float32,
    )


def on_device(panel, ancestor_inverse, diag_inverse, pattern):
    x = lax.axis_index("x")
    zh = lax.axis_index("zh")
    zl = lax.axis_index("zl")
    y = lax.axis_index("y")
    c = lax.axis_index("c")

    moved = lax.ppermute(panel, AXES, turn_pairs())

    def pattern_row(x):
        row = lax.dynamic_slice_in_dim(pattern, (x * 4 + y) * 2 + c, 1, 0)
        return row.astype(jnp.float32).reshape(4, 4, 2)

    row, pair_row = pattern_row(x), pattern_row(x ^ 1)
    mask = jnp.repeat(pick(row, zh, 1), 128, axis=1)[:, None, :]
    masks = [jnp.repeat(pick(r, zl), 128, axis=1)[:, None, :] for r in (row, pair_row)]

    a_cols = lax.all_gather(ancestor_inverse, "c", axis=0)
    a_cols = jnp.concatenate([a_cols[0], a_cols[1]], axis=1)
    a_copies, moved, mask, masks = lax.optimization_barrier(
        (jnp.stack([a_cols] * 4), moved, mask, masks)
    )
    a_all = lax.all_to_all(a_copies, "x", 0, 0, tiled=True).reshape(1024, 256)

    over_zl = lax.all_gather(moved, "zl", axis=0)
    over_zl, a_all = lax.optimization_barrier((over_zl, a_all))
    over_zl = over_zl * mask
    copies = lax.optimization_barrier(jnp.stack([over_zl] * 4))
    by_y = lax.all_to_all(copies, "y", 0, 0, tiled=True)

    moved, _ = lax.optimization_barrier((moved, copies))
    over_zh = lax.all_gather(moved, "zh", axis=0)
    by_y, over_zh = lax.optimization_barrier((by_y, over_zh))
    pair_zh = lax.ppermute(over_zh, "x", [(i, i ^ 1) for i in range(4)])

    partial = sum(
        dot(
            by_y[:, k].reshape(512, 256), a_all[256 * k : 256 * (k + 1)],
            ((1,), (0,)),
        )
        for k in range(4)
    )
    summed = lax.all_to_all(partial, "zh", 0, 0, tiled=True)
    summed = -jnp.sum(summed.reshape(4, 128, 256), axis=0)

    def column(index):
        pair = (over_zh, pair_zh)
        return jnp.concatenate(
            [pick(b, index) * pick(m, index) for b, m in zip(pair, masks)]
        )

    over_zh, pair_zh, _ = lax.optimization_barrier((over_zh, pair_zh, partial))
    pieces = [column(y)] + [
        lax.ppermute(column((y + s) % 4), "y", shift_pairs(s)) for s in (1, 2, 3)
    ]
    pieces = jnp.stack(pieces).reshape(4, 2, 128, 256)
    col_form = jnp.stack([pick(pieces, (y - b) % 4) for b in range(4)], axis=1)
    col_form = col_form.reshape(1024, 256)

    rows = lax.all_gather(summed, "c", axis=0, tiled=True)
    inverse_rows = lax.dynamic_slice_in_dim(rows, c * 128, 128, 1)

    lhs = rows.reshape(4, 4, 2, 8, 256).transpose(1, 2, 0, 3, 4)
    coupling = dot(lhs.reshape(256, 256), col_form, ((1,), (1,)))
    over_y = lax.all_to_all(coupling, ("y", "c"), 0, 0, tiled=True)
    sum_y = jnp.sum(over_y.reshape(4, 2, 4, 8, 1024), axis=0)
    sum_y = sum_y.transpose(1, 0, 2, 3).reshape(64, 1024)
    over_l = lax.all_to_all(sum_y, "zl", 0, 0, tiled=True)
    both = jnp.sum(over_l.reshape(4, 2, 8, 2, 4, 128), axis=0)
    both = both.transpose(2, 1, 3, 0, 4)
    both = jnp.stack([pick(both, (b + x) % 2) for b in range(2)], axis=1)
    return (inverse_rows, diag_inverse - both.reshape(8, 2048))


def solution(mesh):
    fine = Mesh(mesh.devices.reshape(SIZES), AXES)
    prow, pcol = ("x", "zh"), ("zl", "y", "c")
    return jax.shard_map(
        on_device,
        mesh=fine,
        in_specs=(P(pcol, prow), P(prow, pcol), P(AXES, None), P()),
        out_specs=(P(prow, pcol), P(AXES, None)),
        check_vma=False,
    )
```

```python
import jax
import jax.numpy as jnp
from jax import lax
from jax.sharding import Mesh, PartitionSpec as P

AXES = ("x", "zh", "zl", "y", "c")
SIZES = (4, 4, 4, 4, 2)
high = lax.Precision.HIGH


def turn_pairs():
    def flat(x, zh, zl, rest):
        return ((x * 4 + zh) * 4 + zl) * 8 + rest

    return [
        (flat(x, zh, zl, rest), flat(zl, zh, x, rest))
        for x in range(4)
        for zh in range(4)
        for zl in range(4)
        for rest in range(8)
    ]


def shift_pairs(step):
    return [(i, (i + step) % 4) for i in range(4)]


def pick(blocks, index, axis=0):
    return lax.dynamic_index_in_dim(blocks, index, axis, keepdims=False)


def dot(lhs, rhs, dims):
    return lax.dot_general(
        lhs, rhs, (dims, ((), ())), precision=high,
        preferred_element_type=jnp.float32,
    )


def on_device(panel, ancestor_inverse, diag_inverse, pattern):
    x = lax.axis_index("x")
    zh = lax.axis_index("zh")
    zl = lax.axis_index("zl")
    y = lax.axis_index("y")
    c = lax.axis_index("c")

    moved = lax.ppermute(panel, AXES, turn_pairs())

    def pattern_row(x):
        row = lax.dynamic_slice_in_dim(pattern, (x * 4 + y) * 2 + c, 1, 0)
        return row.astype(jnp.float32).reshape(4, 4, 2)

    row, pair_row = pattern_row(x), pattern_row(x ^ 1)
    mask = jnp.repeat(pick(row, zh, 1), 128, axis=1)[:, None, :]
    masks = [jnp.repeat(pick(r, zl), 128, axis=1)[:, None, :] for r in (row, pair_row)]

    a_cols = lax.all_gather(ancestor_inverse, "c", axis=0)
    a_cols = jnp.concatenate([a_cols[0], a_cols[1]], axis=1)
    a_copies, moved, mask, masks = lax.optimization_barrier(
        (jnp.stack([a_cols] * 4), moved, mask, masks)
    )
    a_all = lax.all_to_all(a_copies, "x", 0, 0, tiled=True).reshape(1024, 256)

    over_zl = lax.all_gather(moved, "zl", axis=0)
    over_zl, a_all = lax.optimization_barrier((over_zl, a_all))
    over_zl = over_zl * mask
    copies = lax.optimization_barrier(jnp.stack([over_zl] * 4))
    by_y = lax.all_to_all(copies, "y", 0, 0, tiled=True)

    moved, _ = lax.optimization_barrier((moved, copies))
    over_zh = lax.all_gather(moved, "zh", axis=0)
    by_y, over_zh = lax.optimization_barrier((by_y, over_zh))
    pair_zh = lax.ppermute(over_zh, "x", [(i, i ^ 1) for i in range(4)])

    partial = sum(
        dot(
            by_y[:, k].reshape(512, 256), a_all[256 * k : 256 * (k + 1)],
            ((1,), (0,)),
        )
        for k in range(4)
    )
    summed = lax.all_to_all(partial, "zh", 0, 0, tiled=True)
    summed = -jnp.sum(summed.reshape(4, 128, 256), axis=0)

    def column(index):
        pair = (over_zh, pair_zh)
        return jnp.concatenate(
            [pick(b, index) * pick(m, index) for b, m in zip(pair, masks)]
        )

    over_zh, pair_zh, _ = lax.optimization_barrier((over_zh, pair_zh, partial))
    two, one, three = [
        lax.ppermute(column((y + s) % 4), "y", shift_pairs(s)) for s in (2, 1, 3)
    ]
    pieces = jnp.stack([column(y), one, two, three]).reshape(4, 2, 128, 256)
    col_form = jnp.stack([pick(pieces, (y - b) % 4) for b in range(4)], axis=1)
    col_form = col_form.reshape(1024, 256)

    rows = lax.all_gather(summed, "c", axis=0, tiled=True)
    inverse_rows = lax.dynamic_slice_in_dim(rows, c * 128, 128, 1)

    lhs = rows.reshape(4, 4, 2, 8, 256).transpose(1, 2, 0, 3, 4)
    coupling = dot(lhs.reshape(256, 256), col_form, ((1,), (1,)))
    over_y = lax.all_to_all(coupling, ("y", "c"), 0, 0, tiled=True)
    sum_y = jnp.sum(over_y.reshape(4, 2, 4, 8, 1024), axis=0)
    sum_y = sum_y.transpose(1, 0, 2, 3).reshape(64, 1024)
    over_l = lax.all_to_all(sum_y, "zl", 0, 0, tiled=True)
    both = jnp.sum(over_l.reshape(4, 2, 8, 2, 4, 128), axis=0)
    both = both.transpose(2, 1, 3, 0, 4)
    both = jnp.stack([pick(both, (b + x) % 2) for b in range(2)], axis=1)
    return (inverse_rows, diag_inverse - both.reshape(8, 2048))


def solution(mesh):
    fine = Mesh(mesh.devices.reshape(SIZES), AXES)
    prow, pcol = ("x", "zh"), ("zl", "y", "c")
    return jax.shard_map(
        on_device,
        mesh=fine,
        in_specs=(P(pcol, prow), P(prow, pcol), P(AXES, None), P()),
        out_specs=(P(prow, pcol), P(AXES, None)),
        check_vma=False,
    )
```

```python
import jax
import jax.numpy as jnp
from jax import lax
from jax.sharding import Mesh, PartitionSpec as P

AXES = ("x", "zh", "zl", "y", "c")
SIZES = (4, 4, 4, 4, 2)
high = lax.Precision.HIGH


def turn_pairs():
    def flat(x, zh, zl, rest):
        return ((x * 4 + zh) * 4 + zl) * 8 + rest

    return [
        (flat(x, zh, zl, rest), flat(zl, zh, x, rest))
        for x in range(4)
        for zh in range(4)
        for zl in range(4)
        for rest in range(8)
    ]


def shift_pairs(step):
    return [(i, (i + step) % 4) for i in range(4)]


def pick(blocks, index, axis=0):
    return lax.dynamic_index_in_dim(blocks, index, axis, keepdims=False)


def dot(lhs, rhs, dims):
    return lax.dot_general(
        lhs, rhs, (dims, ((), ())), precision=high,
        preferred_element_type=jnp.float32,
    )


def on_device(panel, ancestor_inverse, diag_inverse, pattern):
    x = lax.axis_index("x")
    zh = lax.axis_index("zh")
    zl = lax.axis_index("zl")
    y = lax.axis_index("y")
    c = lax.axis_index("c")

    moved = lax.ppermute(panel, AXES, turn_pairs())
    own = lax.dynamic_slice(
        pattern, ((x * 4 + y) * 2 + c, (zl * 4 + zh) * 2), (1, 2)
    ).astype(jnp.float32)
    moved = moved * jnp.repeat(own, 128, axis=1)

    a_cols = lax.all_gather(ancestor_inverse, "c", axis=0)
    a_cols = jnp.concatenate([a_cols[0], a_cols[1]], axis=1)
    a_copies, moved = lax.optimization_barrier((jnp.stack([a_cols] * 4), moved))
    a_all = lax.all_to_all(a_copies, "x", 0, 0, tiled=True).reshape(1024, 256)

    over_zl = lax.all_gather(moved, "zl", axis=0)
    over_zl, a_all = lax.optimization_barrier((over_zl, a_all))
    copies = lax.optimization_barrier(jnp.stack([over_zl] * 4))
    by_y = lax.all_to_all(copies, "y", 0, 0, tiled=True)

    moved, _ = lax.optimization_barrier((moved, copies))
    over_zh = lax.all_gather(moved, "zh", axis=0)
    by_y, over_zh = lax.optimization_barrier((by_y, over_zh))
    pair_zh = lax.ppermute(over_zh, "x", [(i, i ^ 1) for i in range(4)])

    partial = sum(
        dot(
            by_y[:, k].reshape(512, 256), a_all[256 * k : 256 * (k + 1)],
            ((1,), (0,)),
        )
        for k in range(4)
    )
    summed = lax.all_to_all(partial, "zh", 0, 0, tiled=True)
    summed = -jnp.sum(summed.reshape(4, 128, 256), axis=0)

    def column(index):
        return jnp.concatenate([pick(over_zh, index), pick(pair_zh, index)])

    over_zh, pair_zh, _ = lax.optimization_barrier((over_zh, pair_zh, partial))
    pieces = [column(y)] + [
        lax.ppermute(column((y + s) % 4), "y", shift_pairs(s)) for s in (1, 2, 3)
    ]
    pieces = jnp.stack(pieces).reshape(4, 2, 128, 256)
    col_form = jnp.stack([pick(pieces, (y - b) % 4) for b in range(4)], axis=1)
    col_form = col_form.reshape(1024, 256)

    rows = lax.all_gather(summed, "c", axis=0, tiled=True)
    inverse_rows = lax.dynamic_slice_in_dim(rows, c * 128, 128, 1)

    lhs = rows.reshape(4, 4, 2, 8, 256).transpose(1, 2, 0, 3, 4)
    coupling = dot(lhs.reshape(256, 256), col_form, ((1,), (1,)))
    over_y = lax.all_to_all(coupling, ("y", "c"), 0, 0, tiled=True)
    sum_y = jnp.sum(over_y.reshape(4, 2, 4, 8, 1024), axis=0)
    sum_y = sum_y.transpose(1, 0, 2, 3).reshape(64, 1024)
    over_l = lax.all_to_all(sum_y, "zl", 0, 0, tiled=True)
    both = jnp.sum(over_l.reshape(4, 2, 8, 2, 4, 128), axis=0)
    both = both.transpose(2, 1, 3, 0, 4)
    both = jnp.stack([pick(both, (b + x) % 2) for b in range(2)], axis=1)
    return (inverse_rows, diag_inverse - both.reshape(8, 2048))


def solution(mesh):
    fine = Mesh(mesh.devices.reshape(SIZES), AXES)
    prow, pcol = ("x", "zh"), ("zl", "y", "c")
    return jax.shard_map(
        on_device,
        mesh=fine,
        in_specs=(P(pcol, prow), P(prow, pcol), P(AXES, None), P()),
        out_specs=(P(prow, pcol), P(AXES, None)),
        check_vma=False,
    )
```
